32 devices in a mesh: leaf: 8 (over y, x, core), panel: 4 (over z).
Axes of the slice: x: 2, y: 2, z: 4, core: 2. Of those that a mesh axis runs over, the one named last changes fastest.
Arguments:
- interior_points: float32 [8, 8, 4096], P('leaf', None, 'panel'), may hold values from -6 to 6
- sep_points: float32 [8, 8, 1024], P('leaf'), may hold values from -6 to 6
- anc_points: float32 [4, 8, 1024], replicated, may hold values from -6 to 6
- scales: float32 [8], replicated, may hold values from 0.8 to 1.6
- block_map: int32 [8, 24], P('leaf', 'panel'), may hold values from 0 to 7, as said below
Outputs:
- factor_cols: float32 [8, 4, 1024, 128], P('leaf', None, 'panel')
- top_front: float32 [8, 1024, 1024], P('leaf', 'panel')
The draws below stay inside these ranges and needn't reach their ends.
Inputs may be any that keep to these rules, and one draw needn't show every extreme that they name: `block_map`: the 6 entries of one interior piece are distinct separator blocks.
All inputs are finite; a program needn't handle non-finite values.
Results may differ from the reference program's by a relative error of at most 0.0001.
Values sent between devices are 32-bit elements; how exact they have to be, the bound alone decides.
No kernel may reach another device: no remote copies, remote signals or barrier semaphores. Data moves between devices by JAX's collectives and lax.ppermute only.
A program may use at most 128 MiB of HBM per device.

```python
import math
import jax
import jax.numpy as jnp
import numpy as np
from jax import lax

S = 1024
BLOCK = 128
NB = 6
LEVELS = 4
DIMS = 8
NI = 1024
LEAVES = 8
PANELS = 4
BLOCKS = 8


def draw_block_map(key, part):
    key_list = jax.random.split(key, LEAVES * PANELS)
    orders = jax.vmap(lambda one_key: jax.random.permutation(one_key, BLOCKS))(key_list)
    return orders[:, :NB].reshape(LEAVES, PANELS * NB).astype(jnp.int32)


def steps_of(rng, shape, cuts, least, high):
    def one(position, shards_of):
        draws = jax.random.uniform(jax.random.fold_in(jax.random.fold_in(rng, 6), position), (shards_of,), jnp.float32, least / len(cuts), high / len(cuts))
        return jnp.repeat(jnp.exp(draws), shape[position] // shards_of).reshape((-1,) + (1,) * (len(shape) - position - 1))

    gain = one(*cuts[0])
    for cut in cuts[1:]:
        gain = gain * one(*cut)
    return gain


def scatter_about(own_key, extent, scale, bound, shards=(), held_as=jnp.bfloat16):
    entries = jax.random.normal(own_key, extent, jnp.float32) * scale
    if len(shards) > 0:
        entries = steps_of(own_key, extent, shards, -0.22, 0.18) * entries
    return jnp.clip(entries, min=-bound, max=bound).astype(held_as)


def setup_inputs(seed: int = 0) -> dict:
    seeds = jax.random.split(jax.random.key(seed), 6)
    interior_points = scatter_about(seeds[0], (LEAVES, DIMS, PANELS * NI), 1.0, 6.0, ((0, 8), (2, 4)), jnp.float32)
    sep_points = scatter_about(seeds[1], (LEAVES, DIMS, S), 1.0, 6.0, ((0, 8),), jnp.float32)
    anc_points = scatter_about(seeds[2], (LEVELS, DIMS, S), 1.0, 6.0, (), jnp.float32)
    scales = jnp.clip(jnp.exp(jax.random.uniform(seeds[3], (DIMS,), jnp.float32, math.log(0.8), math.log(1.6))), 0.8, 1.6)
    block_map = draw_block_map(jax.random.fold_in(seeds[5], 71), 0)
    return {"interior_points": interior_points, "sep_points": sep_points, "anc_points": anc_points, "scales": scales, "block_map": block_map}


NUGGET = 0.5
HIGHEST = lax.Precision.HIGHEST

def kernel(left_pts, right_pts, scales):
    left_scaled = left_pts / scales[:, None]
    right_scaled = right_pts / scales[:, None]
    cross_term = lax.dot_general(left_scaled.astype(jnp.float32), right_scaled.astype(jnp.float32), (((0,), (0,)), ((), ())), precision=HIGHEST, preferred_element_type=jnp.float32)
    distance = jnp.sum(left_scaled * left_scaled, 0)[:, None] + jnp.sum(right_scaled * right_scaled, 0)[None, :] - 2.0 * cross_term
    return jnp.exp(-0.5 * distance)

def with_nugget(matrix, row_start):
    row_ids = row_start + lax.broadcasted_iota(jnp.int32, matrix.shape, 0)
    col_ids = lax.broadcasted_iota(jnp.int32, matrix.shape, 1)
    return matrix + jnp.where(row_ids == col_ids, NUGGET, 0.0).astype(matrix.dtype)

def contribution(points, seps, scales, blocks):
    design = seps.shape[0]
    chosen = seps.reshape(design, -1, BLOCK)[:, blocks, :].reshape(design, -1)
    inner_cov = with_nugget(kernel(points, points, scales), 0)
    factor = jnp.linalg.cholesky(inner_cov)
    solved = jax.scipy.linalg.solve_triangular(factor, kernel(points, chosen, scales), lower=True)
    gram_term = lax.dot_general(solved.astype(jnp.float32), solved.astype(jnp.float32), (((0,), (0,)), ((), ())), precision=HIGHEST, preferred_element_type=jnp.float32)
    return kernel(chosen, chosen, scales) - gram_term

def expand(contrib, blocks, order):
    block_count = blocks.shape[0]
    grid_width = order // BLOCK
    grid_blocks = contrib.reshape(block_count, BLOCK, block_count, BLOCK).transpose(0, 2, 1, 3)
    placed = jnp.zeros((grid_width, grid_width, BLOCK, BLOCK), contrib.dtype).at[blocks[:, None], blocks[None, :]].set(grid_blocks)
    return placed.transpose(0, 2, 1, 3).reshape(order, order)

def pivot_factor(gathered, level_at):
    lowest = level_at * BLOCK
    leading = jnp.linalg.cholesky(gathered[lowest:lowest + BLOCK])
    return jax.scipy.linalg.solve_triangular(leading, gathered.T, lower=True).T

def eliminate(front_rows, cols_all, cols_rows, row_start, level_at):
    update = lax.dot_general(cols_rows.astype(jnp.float32), cols_all.astype(jnp.float32), (((1,), (1,)), ((), ())), precision=HIGHEST, preferred_element_type=jnp.float32)
    lowest = level_at * BLOCK
    row_ids = row_start + lax.broadcasted_iota(jnp.int32, front_rows.shape, 0)
    col_ids = lax.broadcasted_iota(jnp.int32, front_rows.shape, 1)
    inside = (row_ids >= lowest) & (row_ids < lowest + BLOCK) | (col_ids >= lowest) & (col_ids < lowest + BLOCK)
    return jnp.where(inside, 0.0, front_rows - update).astype(front_rows.dtype)

def reference(interior_points, sep_points, anc_points, scales, block_map):
    order = sep_points.shape[2]
    design = sep_points.shape[1]

    def leaf_front(leaf_inputs):
        points, seps, blocks = leaf_inputs
        pieces = points.reshape(design, PANELS, NI).transpose(1, 0, 2)
        maps = blocks.reshape(PANELS, NB)

        def accumulate(total, piece_inputs):
            piece_pts, piece_map = piece_inputs
            return (total + expand(contribution(piece_pts, seps, scales, piece_map), piece_map, order), None)
        summed, unused = lax.scan(accumulate, jnp.zeros((order, order), jnp.float32), (pieces, maps))
        return with_nugget(kernel(seps, seps, scales), 0) + summed
    fronts = lax.map(leaf_front, (interior_points, sep_points, block_map))
    bit_count = LEAVES.bit_length() - 1
    factors = []
    for level_at in range(LEVELS):
        lowest = level_at * BLOCK

        def reduce_front(front_full):
            cols_all = pivot_factor(front_full[:, lowest:lowest + BLOCK], level_at)
            return (eliminate(front_full, cols_all, cols_all, 0, level_at), cols_all)
        reduced, cols_all = lax.map(reduce_front, fronts)
        partner_idx = jnp.asarray(np.arange(LEAVES) ^ 1 << level_at % bit_count).astype(jnp.int32)
        ancestor = with_nugget(kernel(anc_points[level_at], anc_points[level_at], scales), 0)
        fronts = reduced + reduced[partner_idx] + ancestor[None]
        factors.append(cols_all)
    return (jnp.stack(factors, 1), fronts)
```

```python
import jax
import jax.numpy as jnp
from jax import lax
from jax.experimental import pallas as pl
from jax.experimental.pallas import tpu as pltpu
from jax.sharding import PartitionSpec as P

BLOCK = 128
STRIP = 8
NUGGET = 0.5
HIGHEST = lax.Precision.HIGHEST
F32 = jnp.float32
BF16 = jnp.bfloat16
VMEM_LIMIT = 48 * 1024 * 1024


def partner_2(block, axis, apart):
    count = lax.axis_size(axis)
    route = []
    for low in range(count):
        high = low | 1 << apart
        if high != low and high < count:
            route += [(low, high), (high, low)]
    return lax.ppermute(block, axis, route)


def dot_tn(left, right):
    return lax.dot_general(left, right, (((0,), (0,)), ((), ())), preferred_element_type=F32)


def dot_nt_exact(left, right):
    return lax.dot_general(
        left, right, (((1,), (1,)), ((), ())), precision=HIGHEST, preferred_element_type=F32
    )


def halves(value):
    high = value.astype(BF16)
    return high, (value - high.astype(F32)).astype(BF16)


def thirds(value):
    first = value.astype(BF16).astype(F32)
    rest = value - first
    second = rest.astype(BF16).astype(F32)
    return first, second, (rest - second).astype(BF16).astype(F32)


def features(points):
    count = points.shape[1]
    norm = -0.5 * jnp.sum(points * points, 0, keepdims=True)
    norm_parts = [jnp.broadcast_to(part, (STRIP, count)) for part in thirds(norm)]
    row = lax.broadcasted_iota(jnp.int32, (STRIP, count), 0)
    left_norm = jnp.where((row >= 3) & (row < 6), 1.0, 0.0)
    right_norm = jnp.where(row < 3, 1.0, 0.0)
    for at in range(3):
        left_norm = jnp.where(row == at, norm_parts[at], left_norm)
        right_norm = jnp.where(row == at + 3, norm_parts[at], right_norm)
    one, two, three = thirds(points)
    blank = jnp.zeros((STRIP, count), F32)
    left = jnp.concatenate([one, one, two, two, one, three, left_norm, blank], 0)
    right = jnp.concatenate([one, two, one, two, three, one, right_norm, blank], 0)
    return left.astype(BF16), right.astype(BF16)


def spread(part, count):
    return jnp.broadcast_to(part, (STRIP, count))


def inverse_factor(block):
    order = block.shape[0]
    count = order // STRIP
    rest = [block[STRIP * at : STRIP * (at + 1), :] for at in range(count)]
    lane = lax.broadcasted_iota(jnp.int32, (STRIP, order), 1)
    sub = lax.broadcasted_iota(jnp.int32, (STRIP, order), 0)
    work = [jnp.where(lane == sub + STRIP * at, 1.0, 0.0).astype(F32) for at in range(count)]
    done = []
    for top in range(count):
        first = STRIP * top
        rows = [spread(rest[top][m : m + 1, :], order) for m in range(STRIP)]
        unit = [spread(work[top][m : m + 1, :], order) for m in range(STRIP)]
        piv = {}
        for m in range(STRIP):
            for q in range(m, STRIP):
                piv[m, q] = spread(rest[top][m : m + 1, first + q : first + q + 1], order)
        inverse = {}
        strip = None
        for m in range(0, STRIP, 2):
            a, b, c = piv[m, m], piv[m, m + 1], piv[m + 1, m + 1]
            det = a * c - b * b
            inv_det = 1.0 / det
            root = lax.rsqrt(a)
            second = lax.rsqrt(det) * (a * root)
            ia, ib, ic = c * inv_det, -b * inv_det, a * inv_det
            inverse[m] = ia, ib, ic
            lower = unit[m + 1] - b * (root * root) * unit[m]
            for q in range(m + 2, STRIP):
                s0, s1 = piv[m, q], piv[m + 1, q]
                f0, f1 = ia * s0 + ib * s1, ib * s0 + ic * s1
                for z in range(q, STRIP):
                    piv[q, z] = piv[q, z] - (f0 * piv[m, z] + f1 * piv[m + 1, z])
                rows[q] = rows[q] - (f0 * rows[m] + f1 * rows[m + 1])
                unit[q] = unit[q] - (f0 * unit[m] + f1 * unit[m + 1])
            upper = unit[m] * root
            strip = upper if m == 0 else jnp.where(sub == m, upper, strip)
            strip = jnp.where(sub == m + 1, lower * second, strip)
        done.append(strip)
        if top == count - 1:
            break
        row_of = [None] * STRIP
        unit_of = [None] * STRIP
        for m in (6, 4, 2, 0):
            r0, r1, u0, u1 = rows[m], rows[m + 1], unit[m], unit[m + 1]
            for q in range(m + 2, STRIP):
                r0, r1 = r0 - piv[m, q] * row_of[q], r1 - piv[m + 1, q] * row_of[q]
                u0, u1 = u0 - piv[m, q] * unit_of[q], u1 - piv[m + 1, q] * unit_of[q]
            ia, ib, ic = inverse[m]
            row_of[m], row_of[m + 1] = ia * r0 + ib * r1, ib * r0 + ic * r1
            unit_of[m], unit_of[m + 1] = ia * u0 + ib * u1, ib * u0 + ic * u1
        for at in range(top + 1, count):
            column = spread(rest[at][:, first : first + 1], order)
            row_sum, unit_sum = column * row_of[0], column * unit_of[0]
            for m in range(1, STRIP):
                column = spread(rest[at][:, first + m : first + m + 1], order)
                row_sum, unit_sum = row_sum + column * row_of[m], unit_sum + column * unit_of[m]
            rest[at], work[at] = rest[at] - row_sum, work[at] - unit_sum
    return jnp.concatenate(done, 0)


def eye_nugget(order):
    row = lax.broadcasted_iota(jnp.int32, (order, order), 0)
    col = lax.broadcasted_iota(jnp.int32, (order, order), 1)
    return jnp.where(row == col, NUGGET, 0.0).astype(F32)


def schur_kernel(blocks_ref, points_ref, seps_ref, scales_ref, out_ref, left_ref, right_ref, high_ref, low_ref):
    inner = points_ref.shape[1]
    chosen = blocks_ref.shape[0]
    total = inner + chosen * BLOCK
    scales = scales_ref[...]
    left_ref[:, :inner], right_ref[:, :inner] = features(points_ref[...] / scales)
    starts = [pl.multiple_of(blocks_ref[at] * BLOCK, BLOCK) for at in range(chosen)]
    for at in range(chosen):
        lanes = slice(inner + at * BLOCK, inner + (at + 1) * BLOCK)
        left_ref[:, lanes], right_ref[:, lanes] = features(seps_ref[:, pl.ds(starts[at], BLOCK)] / scales)
    out_ref[...] = jnp.zeros_like(out_ref)

    def cov(top, low, high):
        return jnp.exp(dot_tn(left_ref[:, top : top + BLOCK], right_ref[:, low:high]))

    def gram(depth, top, low, high):
        left_high, left_low = high_ref[:depth, top : top + BLOCK], low_ref[:depth, top : top + BLOCK]
        right_high, right_low = high_ref[:depth, low:high], low_ref[:depth, low:high]
        return (
            dot_tn(left_high, right_high)
            + dot_tn(left_high, right_low)
            + dot_tn(left_low, right_high)
        )

    for top in range(0, inner, BLOCK):
        end = top + BLOCK
        pivot = cov(top, top, end) + eye_nugget(BLOCK)
        beside = cov(top, end, total)
        if top > 0:
            pivot = pivot - gram(top, top, top, end)
            beside = beside - gram(top, top, end, total)
        inv_high, inv_low = halves(inverse_factor(pivot))
        beside_high, beside_low = halves(beside)
        solved = (
            jnp.dot(inv_high, beside_high, preferred_element_type=F32)
            + jnp.dot(inv_high, beside_low, preferred_element_type=F32)
            + jnp.dot(inv_low, beside_high, preferred_element_type=F32)
        )
        high_ref[top:end, end:], low_ref[top:end, end:] = halves(solved)
    for at in range(chosen):
        top = inner + at * BLOCK
        strip = cov(top, inner, total) - gram(inner, top, inner, total)
        for to in range(chosen):
            out_ref[pl.ds(starts[at], BLOCK), pl.ds(starts[to], BLOCK)] = strip[:, to * BLOCK : (to + 1) * BLOCK]


def schur(points, seps, scales, blocks):
    inner = points.shape[1]
    order = seps.shape[1]
    total = inner + blocks.shape[0] * BLOCK
    vmem = pl.BlockSpec(memory_space=pltpu.VMEM)
    return pl.pallas_call(
        schur_kernel,
        out_shape=jax.ShapeDtypeStruct((order, order), F32),
        in_specs=[pl.BlockSpec(memory_space=pltpu.SMEM), vmem, vmem, vmem],
        out_specs=vmem,
        scratch_shapes=[
            pltpu.VMEM((8 * STRIP, total), BF16),
            pltpu.VMEM((8 * STRIP, total), BF16),
            pltpu.VMEM((inner, total), BF16),
            pltpu.VMEM((inner, total), BF16),
        ],
        compiler_params=pltpu.CompilerParams(vmem_limit_bytes=VMEM_LIMIT),
        name="schur",
    )(blocks, points, seps, scales)


def covariance_rows(left_pts, right_pts, scales, row_start):
    left_scaled = left_pts / scales
    right_scaled = right_pts / scales
    cross = lax.dot_general(
        left_scaled, right_scaled, (((0,), (0,)), ((), ())), precision=HIGHEST, preferred_element_type=F32
    )
    distance = (
        jnp.sum(left_scaled * left_scaled, 0)[:, None]
        + jnp.sum(right_scaled * right_scaled, 0)[None, :]
        - 2.0 * cross
    )
    row_ids = row_start + lax.broadcasted_iota(jnp.int32, cross.shape, 0)
    col_ids = lax.broadcasted_iota(jnp.int32, cross.shape, 1)
    return jnp.exp(-0.5 * distance) + jnp.where(row_ids == col_ids, NUGGET, 0.0)


def level_kernel(lowest, start_ref, gathered_ref, front_ref, cols_ref, reduced_ref, all_ref):
    start = pl.multiple_of(start_ref[0], STRIP)
    rows = front_ref.shape[0]
    inverse = inverse_factor(gathered_ref[lowest : lowest + BLOCK, :])
    all_ref[...] = dot_nt_exact(gathered_ref[...], inverse)
    cols = all_ref[pl.ds(start, rows), :]
    cols_ref[...] = cols
    update = dot_nt_exact(cols, all_ref[...])
    row_ids = start + lax.broadcasted_iota(jnp.int32, update.shape, 0)
    col_ids = lax.broadcasted_iota(jnp.int32, update.shape, 1)
    inside = (row_ids >= lowest) & (row_ids < lowest + BLOCK) | (col_ids >= lowest) & (
        col_ids < lowest + BLOCK
    )
    reduced_ref[...] = jnp.where(inside, 0.0, front_ref[...] - update)


def level(gathered, front_rows, row_start, lowest):
    def run(*refs):
        level_kernel(lowest, *refs)

    vmem = pl.BlockSpec(memory_space=pltpu.VMEM)
    rows = front_rows.shape[0]
    return pl.pallas_call(
        run,
        out_shape=(
            jax.ShapeDtypeStruct((rows, BLOCK), F32),
            jax.ShapeDtypeStruct(front_rows.shape, F32),
        ),
        in_specs=[pl.BlockSpec(memory_space=pltpu.SMEM), vmem, vmem],
        out_specs=(vmem, vmem),
        scratch_shapes=[pltpu.VMEM(gathered.shape, F32)],
        compiler_params=pltpu.CompilerParams(vmem_limit_bytes=VMEM_LIMIT),
        name="level",
    )(row_start.reshape(1), gathered, front_rows)


def body(interior_points, sep_points, anc_points, scales, block_map):
    order = sep_points.shape[2]
    panels = lax.axis_size("panel")
    row_count = order // panels
    row_start = lax.axis_index("panel") * row_count
    seps = sep_points[0]
    scales = scales[:, None]
    placed = schur(interior_points[0], seps, scales, block_map[0])
    summed = lax.psum_scatter(placed, "panel", scatter_dimension=0, tiled=True)
    local_seps = lax.dynamic_slice_in_dim(seps, row_start, row_count, 1)
    front_rows = covariance_rows(local_seps, seps, scales, row_start) + summed
    levels = anc_points.shape[0]
    ancestors = []
    for level_at in range(levels):
        local_anc = lax.dynamic_slice_in_dim(anc_points[level_at], row_start, row_count, 1)
        ancestors.append(covariance_rows(local_anc, anc_points[level_at], scales, row_start))
    bit_count = lax.axis_size("leaf").bit_length() - 1
    factors = []
    for level_at in range(levels):
        lowest = level_at * BLOCK
        gathered = lax.all_gather(
            front_rows[:, lowest : lowest + BLOCK], "panel", axis=0, tiled=True
        )
        cols_rows, reduced = level(gathered, front_rows, row_start, lowest)
        partner = partner_2(reduced, "leaf", level_at % bit_count)
        front_rows = reduced + partner + ancestors[level_at]
        factors.append(cols_rows)
    return (jnp.stack(factors, 0)[None], front_rows[None])


def solution(mesh):
    in_specs = (P("leaf", None, "panel"), P("leaf", None, None), P(), P(), P("leaf", "panel"))
    out_specs = (P("leaf", None, "panel", None), P("leaf", "panel", None))
    return jax.shard_map(body, mesh=mesh, in_specs=in_specs, out_specs=out_specs, check_vma=False)
```

```python
import jax
import jax.numpy as jnp
from jax import lax
from jax.experimental import pallas as pl
from jax.experimental.pallas import tpu as pltpu
from jax.sharding import PartitionSpec as P

BLOCK = 128
STRIP = 8
LEVEL_COUNT = 4
NUGGET = 0.5
HIGHEST = lax.Precision.HIGHEST
F32 = jnp.float32
BF16 = jnp.bfloat16
VMEM_LIMIT = 48 * 1024 * 1024


def partner_2(block, axis, apart):
    count = lax.axis_size(axis)
    route = []
    for low in range(count):
        high = low | 1 << apart
        if high != low and high < count:
            route += [(low, high), (high, low)]
    return lax.ppermute(block, axis, route)


def dot_tn(left, right):
    return lax.dot_general(left, right, (((0,), (0,)), ((), ())), preferred_element_type=F32)


def dot_nt_exact(left, right):
    return lax.dot_general(
        left, right, (((1,), (1,)), ((), ())), precision=HIGHEST, preferred_element_type=F32
    )


def halves(value):
    high = value.astype(BF16)
    return high, (value - high.astype(F32)).astype(BF16)


def thirds(value):
    first = value.astype(BF16).astype(F32)
    rest = value - first
    second = rest.astype(BF16).astype(F32)
    return first, second, (rest - second).astype(BF16).astype(F32)


def features(points):
    count = points.shape[1]
    norm = -0.5 * jnp.sum(points * points, 0, keepdims=True)
    norm_parts = [jnp.broadcast_to(part, (STRIP, count)) for part in thirds(norm)]
    row = lax.broadcasted_iota(jnp.int32, (STRIP, count), 0)
    left_norm = jnp.where((row >= 3) & (row < 6), 1.0, 0.0)
    right_norm = jnp.where(row < 3, 1.0, 0.0)
    for at in range(3):
        left_norm = jnp.where(row == at, norm_parts[at], left_norm)
        right_norm = jnp.where(row == at + 3, norm_parts[at], right_norm)
    one, two, three = thirds(points)
    blank = jnp.zeros((STRIP, count), F32)
    left = jnp.concatenate([one, one, two, two, one, three, left_norm, blank], 0)
    right = jnp.concatenate([one, two, one, two, three, one, right_norm, blank], 0)
    return left.astype(BF16), right.astype(BF16)


def spread(part, count):
    return jnp.broadcast_to(part, (STRIP, count))


def inverse_steps(block):
    order = block.shape[0]
    count = order // STRIP
    rest = [block[STRIP * at : STRIP * (at + 1), :] for at in range(count)]
    lane = lax.broadcasted_iota(jnp.int32, (STRIP, order), 1)
    sub = lax.broadcasted_iota(jnp.int32, (STRIP, order), 0)
    work = [jnp.where(lane == sub + STRIP * at, 1.0, 0.0).astype(F32) for at in range(count)]
    done = []
    for top in range(count):
        first = STRIP * top
        rows = [spread(rest[top][m : m + 1, :], order) for m in range(STRIP)]
        unit = [spread(work[top][m : m + 1, :], order) for m in range(STRIP)]
        piv = {}
        for m in range(STRIP):
            for q in range(m, STRIP):
                piv[m, q] = spread(rest[top][m : m + 1, first + q : first + q + 1], order)
        inverse = {}
        strip = None
        for m in range(0, STRIP, 2):
            a, b, c = piv[m, m], piv[m, m + 1], piv[m + 1, m + 1]
            det = a * c - b * b
            inv_det = 1.0 / det
            inverse[m] = a, b, c, inv_det
            for q in range(m + 2, STRIP):
                s0, s1 = piv[m, q], piv[m + 1, q]
                f0, f1 = c * s0 - b * s1, a * s1 - b * s0
                for z in range(q, STRIP):
                    piv[q, z] = piv[q, z] - inv_det * (f0 * piv[m, z] + f1 * piv[m + 1, z])
                rows[q] = rows[q] - inv_det * (f0 * rows[m] + f1 * rows[m + 1])
                unit[q] = unit[q] - inv_det * (f0 * unit[m] + f1 * unit[m + 1])
            root = lax.rsqrt(a)
            second = lax.rsqrt(det) * (a * root)
            lower = unit[m + 1] - b * (root * root) * unit[m]
            upper = unit[m] * root
            strip = upper if m == 0 else jnp.where(sub == m, upper, strip)
            strip = jnp.where(sub == m + 1, lower * second, strip)
        done.append(strip)
        if top == count - 1:
            break
        yield None
        row_of = [None] * STRIP
        unit_of = [None] * STRIP
        for m in (6, 4, 2, 0):
            r0, r1, u0, u1 = rows[m], rows[m + 1], unit[m], unit[m + 1]
            for q in range(STRIP - 2, m, -2):
                r0 = r0 - (piv[m, q] * row_of[q] + piv[m, q + 1] * row_of[q + 1])
                r1 = r1 - (piv[m + 1, q] * row_of[q] + piv[m + 1, q + 1] * row_of[q + 1])
                u0 = u0 - (piv[m, q] * unit_of[q] + piv[m, q + 1] * unit_of[q + 1])
                u1 = u1 - (piv[m + 1, q] * unit_of[q] + piv[m + 1, q + 1] * unit_of[q + 1])
            a, b, c, inv_det = inverse[m]
            ia, ib, ic = c * inv_det, b * inv_det, a * inv_det
            row_of[m], row_of[m + 1] = ia * r0 - ib * r1, ic * r1 - ib * r0
            unit_of[m], unit_of[m + 1] = ia * u0 - ib * u1, ic * u1 - ib * u0
        for at in range(top + 1, count):
            for m in (6, 4, 2, 0):
                one = spread(rest[at][:, first + m : first + m + 1], order)
                two = spread(rest[at][:, first + m + 1 : first + m + 2], order)
                row_part = one * row_of[m] + two * row_of[m + 1]
                unit_part = one * unit_of[m] + two * unit_of[m + 1]
                if m == 6:
                    row_left, unit_left = rest[at] - row_part, work[at] - unit_part
                else:
                    row_left, unit_left = row_left - row_part, unit_left - unit_part
            rest[at], work[at] = row_left, unit_left
    yield jnp.concatenate(done, 0)


def inverse_factor(block, beside=()):
    beside = list(beside)
    steps = block.shape[0] // STRIP
    given = 0
    for at, result in enumerate(inverse_steps(block)):
        due = len(beside) * (at + 1) // steps
        for task in beside[given:due]:
            task()
        given = due
    return result


def eye_nugget(order):
    row = lax.broadcasted_iota(jnp.int32, (order, order), 0)
    col = lax.broadcasted_iota(jnp.int32, (order, order), 1)
    return jnp.where(row == col, NUGGET, 0.0).astype(F32)


def schur_kernel(
    blocks_ref, points_ref, seps_ref, scales_ref, out_ref,
    left_ref, right_ref, high_ref, low_ref, across_high_ref, across_low_ref, row_high_ref, row_low_ref, gram_ref,
):
    inner = points_ref.shape[1]
    chosen = blocks_ref.shape[0]
    total = inner + chosen * BLOCK
    scales = scales_ref[...]
    left_ref[:, :inner], right_ref[:, :inner] = features(points_ref[...] / scales)
    starts = [pl.multiple_of(blocks_ref[at] * BLOCK, BLOCK) for at in range(chosen)]
    for at in range(chosen):
        lanes = slice(inner + at * BLOCK, inner + (at + 1) * BLOCK)
        left_ref[:, lanes], right_ref[:, lanes] = features(seps_ref[:, pl.ds(starts[at], BLOCK)] / scales)
    out_ref[...] = jnp.zeros_like(out_ref)

    def cov(top, low, high):
        return jnp.exp(dot_tn(left_ref[:, top : top + BLOCK], right_ref[:, low:high]))

    def dot(left, right):
        return jnp.dot(left, right, preferred_element_type=F32)

    def gram(top, low, high, begin, depth):
        deep = slice(begin, depth)
        left_high, left_low = across_high_ref[top : top + BLOCK, deep], across_low_ref[top : top + BLOCK, deep]
        right_high, right_low = high_ref[deep, low:high], low_ref[deep, low:high]
        return dot(left_high, right_high) + dot(left_high, right_low) + dot(left_low, right_high)

    def prepare(top, low, high):
        value = cov(top, low, high)
        if top > 0:
            value = value - gram(top, low, high, 0, top)
        row_high_ref[:, low:high], row_low_ref[:, low:high] = halves(value)

    def solve(top, inv_high, inv_low, low, high):
        end = top + BLOCK
        row_high, row_low = row_high_ref[:, low:high], row_low_ref[:, low:high]
        value = dot(inv_high, row_high) + dot(inv_high, row_low) + dot(inv_low, row_high)
        high_ref[top:end, low:high], low_ref[top:end, low:high] = halves(value)
        across_high_ref[low:high, top:end], across_low_ref[low:high, top:end] = halves(value.T)

    def partial(at, low, high, depth):
        top = inner + at * BLOCK
        lanes = slice(low - inner, high - inner)
        rows = slice(at * BLOCK, (at + 1) * BLOCK)
        gram_ref[rows, lanes] = cov(top, low, high) - gram(top, low, high, 0, depth)

    def tiles(begin, wide):
        first = [(begin, begin + BLOCK)] if (total - begin) % wide else []
        begin += BLOCK * len(first)
        return first + [(at, at + wide) for at in range(begin, total, wide)]

    waiting = []
    for top in range(0, inner, BLOCK):
        end = top + BLOCK
        pivot = cov(top, top, end) + eye_nugget(BLOCK)
        if top > 0:
            pivot = pivot - gram(top, top, end, 0, top)
        tasks = []
        for low, high in tiles(end, 2 * BLOCK):
            tasks += [lambda job=job, low=low, high=high: job(low, high) for job in waiting]
            tasks.append(lambda low=low, high=high: prepare(top, low, high))
        if end == inner:
            for at in range(chosen):
                for low, high in tiles(inner, 3 * BLOCK):
                    tasks.append(lambda at=at, low=low, high=high: partial(at, low, high, top))
        inv_high, inv_low = halves(inverse_factor(pivot, tasks))
        if end < inner:
            solve(top, inv_high, inv_low, end, end + BLOCK)
            waiting = [lambda low, high, top=top, one=inv_high, two=inv_low: solve(top, one, two, low, high)]
        else:
            for low, high in tiles(end, 2 * BLOCK):
                solve(top, inv_high, inv_low, low, high)
    for at in range(chosen):
        top = inner + at * BLOCK
        rows = slice(at * BLOCK, (at + 1) * BLOCK)
        strip = gram_ref[rows, :] - gram(top, inner, total, inner - BLOCK, inner)
        for to in range(chosen):
            out_ref[pl.ds(starts[at], BLOCK), pl.ds(starts[to], BLOCK)] = strip[:, to * BLOCK : (to + 1) * BLOCK]


def schur_scratch(inner, total):
    return [
        pltpu.VMEM((8 * STRIP, total), BF16),
        pltpu.VMEM((8 * STRIP, total), BF16),
        pltpu.VMEM((inner, total), BF16),
        pltpu.VMEM((inner, total), BF16),
        pltpu.VMEM((total, inner), BF16),
        pltpu.VMEM((total, inner), BF16),
        pltpu.VMEM((BLOCK, total), BF16),
        pltpu.VMEM((BLOCK, total), BF16),
        pltpu.VMEM((total - inner, total - inner), F32),
    ]


def schur(points, seps, scales, blocks):
    inner = points.shape[1]
    order = seps.shape[1]
    total = inner + blocks.shape[0] * BLOCK
    vmem = pl.BlockSpec(memory_space=pltpu.VMEM)
    return pl.pallas_call(
        schur_kernel,
        out_shape=jax.ShapeDtypeStruct((order, order), F32),
        in_specs=[pl.BlockSpec(memory_space=pltpu.SMEM), vmem, vmem, vmem],
        out_specs=vmem,
        scratch_shapes=schur_scratch(inner, total),
        compiler_params=pltpu.CompilerParams(vmem_limit_bytes=VMEM_LIMIT),
        name="schur",
    )(blocks, points, seps, scales)


def covariance_rows(left_pts, right_pts, scales, row_start):
    left_scaled = left_pts / scales
    right_scaled = right_pts / scales
    cross = lax.dot_general(
        left_scaled, right_scaled, (((0,), (0,)), ((), ())), precision=HIGHEST, preferred_element_type=F32
    )
    distance = (
        jnp.sum(left_scaled * left_scaled, 0)[:, None]
        + jnp.sum(right_scaled * right_scaled, 0)[None, :]
        - 2.0 * cross
    )
    row_ids = row_start + lax.broadcasted_iota(jnp.int32, cross.shape, 0)
    col_ids = lax.broadcasted_iota(jnp.int32, cross.shape, 1)
    return jnp.exp(-0.5 * distance) + jnp.where(row_ids == col_ids, NUGGET, 0.0)


def level_kernel(lowest, start_ref, gathered_ref, front_ref, cols_ref, reduced_ref, all_ref):
    start = pl.multiple_of(start_ref[0], STRIP)
    rows = front_ref.shape[0]
    inverse = inverse_factor(gathered_ref[lowest : lowest + BLOCK, :])
    all_ref[...] = dot_nt_exact(gathered_ref[...], inverse)
    cols = all_ref[pl.ds(start, rows), :]
    cols_ref[...] = cols
    update = dot_nt_exact(cols, all_ref[...])
    row_ids = start + lax.broadcasted_iota(jnp.int32, update.shape, 0)
    col_ids = lax.broadcasted_iota(jnp.int32, update.shape, 1)
    inside = (row_ids >= lowest) & (row_ids < lowest + BLOCK) | (col_ids >= lowest) & (
        col_ids < lowest + BLOCK
    )
    reduced_ref[...] = jnp.where(inside, 0.0, front_ref[...] - update)


def level(gathered, front_rows, row_start, lowest):
    def run(*refs):
        level_kernel(lowest, *refs)

    vmem = pl.BlockSpec(memory_space=pltpu.VMEM)
    rows = front_rows.shape[0]
    return pl.pallas_call(
        run,
        out_shape=(
            jax.ShapeDtypeStruct((rows, BLOCK), F32),
            jax.ShapeDtypeStruct(front_rows.shape, F32),
        ),
        in_specs=[pl.BlockSpec(memory_space=pltpu.SMEM), vmem, vmem],
        out_specs=(vmem, vmem),
        scratch_shapes=[pltpu.VMEM(gathered.shape, F32)],
        compiler_params=pltpu.CompilerParams(vmem_limit_bytes=VMEM_LIMIT),
        name="level",
    )(row_start.reshape(1), gathered, front_rows)


def schur_split_kernel(blocks_ref, points_ref, seps_ref, scales_ref, first_ref, next_ref, rest_ref, last_ref, sum_ref, *scratch):
    schur_kernel(blocks_ref, points_ref, seps_ref, scales_ref, sum_ref, *scratch)
    half = LEVEL_COUNT * BLOCK
    first_ref[...] = sum_ref[:, :BLOCK]
    next_ref[...] = sum_ref[BLOCK:, BLOCK : 2 * BLOCK]
    rest_ref[...] = sum_ref[2 * BLOCK :, 2 * BLOCK : half]
    last_ref[...] = sum_ref[half:, half:]


def schur_split(points, seps, scales, blocks):
    inner = points.shape[1]
    order = seps.shape[1]
    half = LEVEL_COUNT * BLOCK
    total = inner + blocks.shape[0] * BLOCK
    vmem = pl.BlockSpec(memory_space=pltpu.VMEM)
    return pl.pallas_call(
        schur_split_kernel,
        out_shape=(
            jax.ShapeDtypeStruct((order, BLOCK), F32),
            jax.ShapeDtypeStruct((order - BLOCK, BLOCK), F32),
            jax.ShapeDtypeStruct((order - 2 * BLOCK, half - 2 * BLOCK), F32),
            jax.ShapeDtypeStruct((order - half, order - half), F32),
        ),
        in_specs=[pl.BlockSpec(memory_space=pltpu.SMEM), vmem, vmem, vmem],
        out_specs=(vmem, vmem, vmem, vmem),
        scratch_shapes=[pltpu.VMEM((order, order), F32)] + schur_scratch(inner, total),
        compiler_params=pltpu.CompilerParams(vmem_limit_bytes=VMEM_LIMIT),
        name="schur",
    )(blocks, points, seps, scales)


def clear_rows(value, block_at):
    row_ids = lax.broadcasted_iota(jnp.int32, value.shape, 0)
    low = block_at * BLOCK
    return jnp.where((row_ids >= low) & (row_ids < low + BLOCK), 0.0, value)


def rows_of(ref, block_at):
    return ref[block_at * BLOCK : (block_at + 1) * BLOCK, :]


def dot_nt(left, right):
    left_high, left_low = halves(left)
    right_high, right_low = halves(right)

    def product(one, two):
        return lax.dot_general(one, two, (((1,), (1,)), ((), ())), preferred_element_type=F32)

    return product(left_high, right_high) + product(left_high, right_low) + product(left_low, right_high)


def covariance_block(rows, cols, shift):
    value = jnp.exp(dot_tn(features(rows)[0], features(cols)[1]))
    row_ids = lax.broadcasted_iota(jnp.int32, value.shape, 0)
    col_ids = lax.broadcasted_iota(jnp.int32, value.shape, 1)
    return value + jnp.where(row_ids == col_ids + shift, NUGGET, 0.0)


def column_covariance(points, block_at):
    return covariance_block(points, points[:, block_at * BLOCK : (block_at + 1) * BLOCK], block_at * BLOCK)


def below(value, blocks):
    return jnp.concatenate([jnp.zeros((blocks * BLOCK, value.shape[1]), F32), value], 0)


def level0_kernel(seps_ref, scales_ref, sum_ref, factor_ref):
    column = column_covariance(seps_ref[...] / scales_ref[...], 0) + sum_ref[...]
    factor_ref[...] = dot_nt_exact(column, inverse_factor(column[:BLOCK]))


def first_column(block_at, summed, seps_ref, other_seps_ref, anc_ref, scales_ref, mine_ref, other_ref):
    scales = scales_ref[...]
    value = (
        summed
        + column_covariance(seps_ref[...] / scales, block_at)
        + column_covariance(other_seps_ref[...] / scales, block_at)
        - dot_nt(mine_ref[...], rows_of(mine_ref, block_at))
        - dot_nt(other_ref[...], rows_of(other_ref, block_at))
    )
    return clear_rows(value, 0) + column_covariance(anc_ref[...] / scales, block_at)


def level1_kernel(sum_ref, *refs):
    *refs, factor_ref = refs
    column = first_column(1, below(sum_ref[...], 1), *refs)
    factor_ref[...] = dot_nt_exact(column, inverse_factor(column[BLOCK : 2 * BLOCK]))


def next_kernel(factor_ref, sum_ref, *refs):
    *refs, out_ref = refs
    column = first_column(2, below(sum_ref[:, :BLOCK], 2), *refs)
    out_ref[...] = clear_rows(column - dot_nt(factor_ref[...], rows_of(factor_ref, 2)), 1)


def share_kernel(place_ref, factor_ref, sum_ref, last_ref, *refs):
    *refs, third_ref, own_ref = refs
    seps_ref, other_seps_ref, anc_ref, scales_ref, mine_ref, other_ref = refs
    column = first_column(3, below(sum_ref[:, BLOCK:], 2), *refs)
    third_ref[...] = clear_rows(column - dot_nt(factor_ref[...], rows_of(factor_ref, 3)), 1)
    at = place_ref[0]
    half = LEVEL_COUNT * BLOCK
    scales = scales_ref[...]
    anc = anc_ref[...] / scales

    @pl.when(at < LEVEL_COUNT)
    def _():
        zero = clear_rows(
            column_covariance(anc, 0) - dot_nt(factor_ref[...], rows_of(factor_ref, 0)), 1
        )
        own_ref[...] = jnp.where(at == 0, zero, jnp.where(at == 3, third_ref[...], 0.0))

    @pl.when(at >= LEVEL_COUNT)
    def _():
        lanes = pl.ds(pl.multiple_of(at * BLOCK, BLOCK), BLOCK)
        anc_here = anc_ref[:, lanes] / scales
        tail = slice(half, None)
        here = factor_ref[lanes, :]
        top = covariance_block(anc[:, :BLOCK], anc_here, -half - BLOCK)
        own_ref[:BLOCK, :] = top - dot_nt(factor_ref[:BLOCK, :], here)
        own_ref[BLOCK : 3 * BLOCK, :] = jnp.zeros((2 * BLOCK, BLOCK), F32)
        own_ref[3 * BLOCK : half, :] = third_ref[lanes, :].T
        shift = at * BLOCK - half
        value = last_ref[...] + covariance_block(anc[:, tail], anc_here, shift)
        value = value - dot_nt(factor_ref[tail, :], here)
        for points_ref in (seps_ref, other_seps_ref):
            value = value + covariance_block(points_ref[:, tail] / scales, points_ref[:, lanes] / scales, shift)
        for one_ref in (mine_ref, other_ref):
            value = value - dot_nt(one_ref[tail, :], one_ref[lanes, :])
        own_ref[tail, :] = value


def level2_kernel(mine_ref, other_ref, anc_ref, scales_ref, factor_ref):
    column = mine_ref[...] + other_ref[...] + column_covariance(anc_ref[...] / scales_ref[...], 2)
    factor_ref[...] = dot_nt_exact(column, inverse_factor(column[2 * BLOCK : 3 * BLOCK]))


def level3_kernel(sum_ref, anc1_ref, anc2_ref, scales_ref, mine_ref, other_ref, factor_ref):
    scales = scales_ref[...]
    value = (
        sum_ref[...]
        + 2.0 * column_covariance(anc1_ref[...] / scales, 3)
        - dot_nt(mine_ref[...], rows_of(mine_ref, 3))
        - dot_nt(other_ref[...], rows_of(other_ref, 3))
    )
    column = clear_rows(value, 2) + column_covariance(anc2_ref[...] / scales, 3)
    factor_ref[...] = dot_nt_exact(column, inverse_factor(column[3 * BLOCK : 4 * BLOCK]))


def top_kernel(start_ref, sum_ref, ancs_ref, scales_ref, mine_ref, other_ref, last_ref, out_ref):
    start = pl.multiple_of(start_ref[0], BLOCK)
    shape = out_ref.shape
    scales = scales_ref[...]
    row_ids = start + lax.broadcasted_iota(jnp.int32, shape, 0)
    col_ids = lax.broadcasted_iota(jnp.int32, shape, 1)

    def inside(block_at):
        low, high = block_at * BLOCK, (block_at + 1) * BLOCK
        return (row_ids >= low) & (row_ids < high) | (col_ids >= low) & (col_ids < high)

    def ancestor(level_at):
        rows = ancs_ref[level_at, :, pl.ds(start, shape[0])] / scales
        return covariance_block(rows, ancs_ref[level_at] / scales, -start)

    def product(ref):
        return dot_nt(ref[pl.ds(start, shape[0]), :], ref[...])

    summed = jnp.concatenate(
        [sum_ref[core, side, pair] for pair in range(2) for core in range(2) for side in range(2)], 1
    )
    value = summed + 2.0 * ancestor(1) - product(mine_ref) - product(other_ref)
    value = jnp.where(inside(2), 0.0, value) + ancestor(2) - product(last_ref)
    out_ref[...] = 2.0 * jnp.where(inside(3), 0.0, value) + ancestor(3)


def local_call(kernel, name, shapes, *operands, scalar=None, micros=2):
    vmem = pl.BlockSpec(memory_space=pltpu.VMEM)
    in_specs = [vmem] * len(operands)
    if scalar is not None:
        in_specs = [pl.BlockSpec(memory_space=pltpu.SMEM)] + in_specs
        operands = (scalar.reshape(1),) + operands
    outs = tuple(jax.ShapeDtypeStruct(shape, F32) for shape in shapes)
    return pl.pallas_call(
        kernel,
        out_shape=outs,
        in_specs=in_specs,
        out_specs=(vmem,) * len(outs),
        compiler_params=pltpu.CompilerParams(vmem_limit_bytes=VMEM_LIMIT),
        cost_estimate=pl.CostEstimate(flops=micros * 10**9, bytes_accessed=2**20, transcendentals=0),
        name=name,
    )(*operands)


def cut(value, start, size, axis=0):
    return lax.dynamic_slice_in_dim(value, start, size, axis)


def grouped_body(interior_points, sep_points, anc_points, scales, block_map):
    order = sep_points.shape[2]
    design = sep_points.shape[1]
    inner = interior_points.shape[2]
    chosen = block_map.shape[1]
    leaves, panels = lax.axis_size("leaf"), lax.axis_size("panel")
    place, panel = lax.axis_index("leaf"), lax.axis_index("panel")
    core, side, pair = place % 2, place // 2 % 2, place // 4
    half, rows = order // 2, order // panels
    scales = scales[:, None]
    tall = [(order, BLOCK)]

    def flip(value, bit):
        return lax.ppermute(value, "leaf", [(at, at ^ bit) for at in range(leaves)])

    def across(value, bit):
        return lax.ppermute(value, "panel", [(at, at ^ bit) for at in range(panels)])

    def target(leaf, piece):
        return (4 * (leaf % 2) + piece) * panels + leaf // 2

    def route(change):
        return [
            (leaf * panels + piece, target(leaf ^ change, piece))
            for leaf in range(leaves)
            for piece in range(panels)
        ]

    def share(part):
        other = flip(part, 1)
        return jnp.where(core == 0, jnp.concatenate([part, other]), jnp.concatenate([other, part]))

    def my_half(value):
        size = value.shape[0] // 2
        return cut(value, core * size, size)

    def core_sum(value):
        size = value.shape[0] // 2
        return my_half(value) + flip(cut(value, (1 - core) * size, size), 1)

    def group_sum(part, bits):
        for bit in bits:
            part = part + flip(part, bit)
        return share(part)

    names = jnp.pad(block_map.astype(F32), ((0, design - 1), (0, BLOCK - chosen)))
    packed = jnp.concatenate([interior_points[0], sep_points[0], names], 1)
    packed = lax.ppermute(packed, ("leaf", "panel"), route(0))
    points, seps = packed[:, :inner], packed[:, inner : inner + order]
    blocks = packed[0, inner + order : inner + order + chosen].astype(jnp.int32)
    first, second, rest, last = schur_split(points, seps, scales, blocks)
    other_seps = lax.ppermute(sep_points[0], ("leaf", "panel"), route(1))

    first, second, rest, last = lax.optimization_barrier((core_sum(first), second, rest, last))
    first = group_sum(first, (2,))
    (factor0,) = local_call(level0_kernel, "level0", tall, seps, scales, first)
    second = group_sum(core_sum(second), (2, 4))
    rest = group_sum(core_sum(rest), (4, 2))
    other0 = share(flip(my_half(factor0), 4))
    shared = (seps, other_seps, anc_points[0], scales, factor0, other0)
    (factor1,) = local_call(level1_kernel, "level1", tall, second, *shared)
    (reduced2,) = local_call(next_kernel, "next1", tall, factor1, rest, *shared)
    arrived2 = share(across(my_half(reduced2), 1))
    width = (order - half) // 2
    piece = cut(last, core * width, width, 1) + flip(cut(last, (1 - core) * width, width, 1), 1)
    width //= 2
    piece = cut(piece, side * width, width, 1) + flip(cut(piece, (1 - side) * width, width, 1), 2)
    piece = piece + flip(piece, 4)
    column_at = 4 * pair + 2 * core + side
    reduced3, own = local_call(
        share_kernel, "share1", tall + tall, factor1, rest, piece, *shared, scalar=column_at
    )
    summed3 = my_half(reduced3)
    summed3 = summed3 + across(summed3, 1)
    (factor2,) = local_call(level2_kernel, "level2", tall, reduced2, arrived2, anc_points[1], scales)
    summed3 = share(summed3 + across(summed3, 2))
    partner2 = share(across(my_half(factor2), 2))
    (factor3,) = local_call(
        level3_kernel, "level3", tall, summed3, anc_points[1], anc_points[2], scales, factor2, partner2
    )
    own = lax.psum_scatter(own, "panel", scatter_dimension=0, tiled=True)
    for at, bit in ((pair, 4), (side, 2), (core, 1)):
        other = flip(own, bit)
        own = jnp.where(at == 0, jnp.stack([own, other]), jnp.stack([other, own]))
    start = panel * rows
    (top,) = local_call(
        top_kernel,
        "top",
        [(rows, order)],
        own,
        anc_points,
        scales,
        factor2,
        partner2,
        factor3,
        scalar=start,
    )
    piece_at = (place % 4) * rows
    early = lax.ppermute(
        jnp.stack([cut(factor0, piece_at, rows), cut(factor1, piece_at, rows)]),
        ("leaf", "panel"),
        [(at, to) for to, at in route(0)],
    )
    late = jnp.stack([cut(jnp.where(panel // 2 == pair, factor2, partner2), start, rows), cut(factor3, start, rows)])
    return (jnp.concatenate([early, late])[None], top[None])


def body(interior_points, sep_points, anc_points, scales, block_map):
    order = sep_points.shape[2]
    panels = lax.axis_size("panel")
    row_count = order // panels
    row_start = lax.axis_index("panel") * row_count
    seps = sep_points[0]
    scales = scales[:, None]
    placed = schur(interior_points[0], seps, scales, block_map[0])
    summed = lax.psum_scatter(placed, "panel", scatter_dimension=0, tiled=True)
    local_seps = lax.dynamic_slice_in_dim(seps, row_start, row_count, 1)
    front_rows = covariance_rows(local_seps, seps, scales, row_start) + summed
    levels = anc_points.shape[0]
    ancestors = []
    for level_at in range(levels):
        local_anc = lax.dynamic_slice_in_dim(anc_points[level_at], row_start, row_count, 1)
        ancestors.append(covariance_rows(local_anc, anc_points[level_at], scales, row_start))
    bit_count = lax.axis_size("leaf").bit_length() - 1
    factors = []
    for level_at in range(levels):
        lowest = level_at * BLOCK
        gathered = lax.all_gather(
            front_rows[:, lowest : lowest + BLOCK], "panel", axis=0, tiled=True
        )
        cols_rows, reduced = level(gathered, front_rows, row_start, lowest)
        partner = partner_2(reduced, "leaf", level_at % bit_count)
        front_rows = reduced + partner + ancestors[level_at]
        factors.append(cols_rows)
    return (jnp.stack(factors, 0)[None], front_rows[None])


def solution(mesh):
    in_specs = (P("leaf", None, "panel"), P("leaf", None, None), P(), P(), P("leaf", "panel"))
    out_specs = (P("leaf", None, "panel", None), P("leaf", "panel", None))
    sizes = mesh.shape["leaf"], mesh.shape["panel"]
    chosen = grouped_body if sizes == (8, 4) else body
    return jax.shard_map(chosen, mesh=mesh, in_specs=in_specs, out_specs=out_specs, check_vma=False)
```

```python
import jax
import jax.numpy as jnp
from jax import lax
from jax.experimental import pallas as pl
from jax.experimental.pallas import tpu as pltpu
from jax.sharding import PartitionSpec as P

BLOCK = 128
STRIP = 8
LEVEL_COUNT = 4
NUGGET = 0.5
HIGHEST = lax.Precision.HIGHEST
F32 = jnp.float32
BF16 = jnp.bfloat16
VMEM_LIMIT = 48 * 1024 * 1024


def partner_2(block, axis, apart):
    count = lax.axis_size(axis)
    route = []
    for low in range(count):
        high = low | 1 << apart
        if high != low and high < count:
            route += [(low, high), (high, low)]
    return lax.ppermute(block, axis, route)


def dot_tn(left, right):
    return lax.dot_general(left, right, (((0,), (0,)), ((), ())), preferred_element_type=F32)


def dot_nt_exact(left, right):
    return lax.dot_general(
        left, right, (((1,), (1,)), ((), ())), precision=HIGHEST, preferred_element_type=F32
    )


def halves(value):
    high = value.astype(BF16)
    return high, (value - high.astype(F32)).astype(BF16)


def thirds(value):
    first = value.astype(BF16).astype(F32)
    rest = value - first
    second = rest.astype(BF16).astype(F32)
    return first, second, (rest - second).astype(BF16).astype(F32)


def features(points):
    count = points.shape[1]
    norm = -0.5 * jnp.sum(points * points, 0, keepdims=True)
    norm_parts = [jnp.broadcast_to(part, (STRIP, count)) for part in thirds(norm)]
    row = lax.broadcasted_iota(jnp.int32, (STRIP, count), 0)
    left_norm = jnp.where((row >= 3) & (row < 6), 1.0, 0.0)
    right_norm = jnp.where(row < 3, 1.0, 0.0)
    for at in range(3):
        left_norm = jnp.where(row == at, norm_parts[at], left_norm)
        right_norm = jnp.where(row == at + 3, norm_parts[at], right_norm)
    one, two, three = thirds(points)
    blank = jnp.zeros((STRIP, count), F32)
    left = jnp.concatenate([one, one, two, two, one, three, left_norm, blank], 0)
    right = jnp.concatenate([one, two, one, two, three, one, right_norm, blank], 0)
    return left.astype(BF16), right.astype(BF16)


def spread(part, count):
    return jnp.broadcast_to(part, (STRIP, count))


def inverse_steps(block):
    order = block.shape[0]
    count = order // STRIP
    rest = [block[STRIP * at : STRIP * (at + 1), :] for at in range(count)]
    lane = lax.broadcasted_iota(jnp.int32, (STRIP, order), 1)
    sub = lax.broadcasted_iota(jnp.int32, (STRIP, order), 0)
    work = [jnp.where(lane == sub + STRIP * at, 1.0, 0.0).astype(F32) for at in range(count)]
    done = []
    for top in range(count):
        first = STRIP * top
        rows = [spread(rest[top][m : m + 1, :], order) for m in range(STRIP)]
        unit = [spread(work[top][m : m + 1, :], order) for m in range(STRIP)]
        piv = {}
        for m in range(STRIP):
            for q in range(m, STRIP):
                piv[m, q] = spread(rest[top][m : m + 1, first + q : first + q + 1], order)
        inverse = {}
        strip = None
        for m in range(0, STRIP, 2):
            a, b, c = piv[m, m], piv[m, m + 1], piv[m + 1, m + 1]
            det = a * c - b * b
            inv_det = 1.0 / det
            inverse[m] = a, b, c, inv_det
            for q in range(m + 2, STRIP):
                s0, s1 = piv[m, q], piv[m + 1, q]
                f0, f1 = c * s0 - b * s1, a * s1 - b * s0
                for z in range(q, STRIP):
                    piv[q, z] = piv[q, z] - inv_det * (f0 * piv[m, z] + f1 * piv[m + 1, z])
                rows[q] = rows[q] - inv_det * (f0 * rows[m] + f1 * rows[m + 1])
                unit[q] = unit[q] - inv_det * (f0 * unit[m] + f1 * unit[m + 1])
            root = lax.rsqrt(a)
            second = lax.rsqrt(det) * (a * root)
            lower = unit[m + 1] - b * (root * root) * unit[m]
            upper = unit[m] * root
            strip = upper if m == 0 else jnp.where(sub == m, upper, strip)
            strip = jnp.where(sub == m + 1, lower * second, strip)
        done.append(strip)
        if top == count - 1:
            break
        yield None
        row_of = [None] * STRIP
        unit_of = [None] * STRIP
        for m in (6, 4, 2, 0):
            r0, r1, u0, u1 = rows[m], rows[m + 1], unit[m], unit[m + 1]
            for q in range(STRIP - 2, m, -2):
                r0 = r0 - (piv[m, q] * row_of[q] + piv[m, q + 1] * row_of[q + 1])
                r1 = r1 - (piv[m + 1, q] * row_of[q] + piv[m + 1, q + 1] * row_of[q + 1])
                u0 = u0 - (piv[m, q] * unit_of[q] + piv[m, q + 1] * unit_of[q + 1])
                u1 = u1 - (piv[m + 1, q] * unit_of[q] + piv[m + 1, q + 1] * unit_of[q + 1])
            a, b, c, inv_det = inverse[m]
            ia, ib, ic = c * inv_det, b * inv_det, a * inv_det
            row_of[m], row_of[m + 1] = ia * r0 - ib * r1, ic * r1 - ib * r0
            unit_of[m], unit_of[m + 1] = ia * u0 - ib * u1, ic * u1 - ib * u0
        for at in range(top + 1, count):
            for m in (6, 4, 2, 0):
                one = spread(rest[at][:, first + m : first + m + 1], order)
                two = spread(rest[at][:, first + m + 1 : first + m + 2], order)
                row_part = one * row_of[m] + two * row_of[m + 1]
                unit_part = one * unit_of[m] + two * unit_of[m + 1]
                if m == 6:
                    row_left, unit_left = rest[at] - row_part, work[at] - unit_part
                else:
                    row_left, unit_left = row_left - row_part, unit_left - unit_part
            rest[at], work[at] = row_left, unit_left
    yield jnp.concatenate(done, 0)


def inverse_factor(block, beside=()):
    beside = list(beside)
    steps = block.shape[0] // STRIP
    given = 0
    for at, result in enumerate(inverse_steps(block)):
        due = len(beside) * (at + 1) // steps
        for task in beside[given:due]:
            task()
        given = due
    return result


def eye_nugget(order):
    row = lax.broadcasted_iota(jnp.int32, (order, order), 0)
    col = lax.broadcasted_iota(jnp.int32, (order, order), 1)
    return jnp.where(row == col, NUGGET, 0.0).astype(F32)


def schur_kernel(
    blocks_ref, points_ref, seps_ref, scales_ref, out_ref,
    left_ref, right_ref, high_ref, low_ref, across_high_ref, across_low_ref, row_high_ref, row_low_ref, gram_ref,
):
    inner = points_ref.shape[1]
    chosen = blocks_ref.shape[0]
    total = inner + chosen * BLOCK
    scales = scales_ref[...]
    left_ref[:, :inner], right_ref[:, :inner] = features(points_ref[...] / scales)
    starts = [pl.multiple_of(blocks_ref[at] * BLOCK, BLOCK) for at in range(chosen)]
    for at in range(chosen):
        lanes = slice(inner + at * BLOCK, inner + (at + 1) * BLOCK)
        left_ref[:, lanes], right_ref[:, lanes] = features(seps_ref[:, pl.ds(starts[at], BLOCK)] / scales)
    out_ref[...] = jnp.zeros_like(out_ref)

    def cov(top, low, high):
        return jnp.exp(dot_tn(left_ref[:, top : top + BLOCK], right_ref[:, low:high]))

    def dot(left, right):
        return jnp.dot(left, right, preferred_element_type=F32)

    def gram(top, low, high, begin, depth):
        deep = slice(begin, depth)
        left_high, left_low = across_high_ref[top : top + BLOCK, deep], across_low_ref[top : top + BLOCK, deep]
        right_high, right_low = high_ref[deep, low:high], low_ref[deep, low:high]
        return dot(left_high, right_high) + dot(left_high, right_low) + dot(left_low, right_high)

    def prepare(top, low, high):
        value = cov(top, low, high)
        if top > 0:
            value = value - gram(top, low, high, 0, top)
        row_high_ref[:, low:high], row_low_ref[:, low:high] = halves(value)

    def solve(top, inv_high, inv_low, low, high):
        end = top + BLOCK
        row_high, row_low = row_high_ref[:, low:high], row_low_ref[:, low:high]
        value = dot(inv_high, row_high) + dot(inv_high, row_low) + dot(inv_low, row_high)
        high_ref[top:end, low:high], low_ref[top:end, low:high] = halves(value)
        across_high_ref[low:high, top:end], across_low_ref[low:high, top:end] = halves(value.T)

    def partial(at, low, high, depth):
        top = inner + at * BLOCK
        lanes = slice(low - inner, high - inner)
        rows = slice(at * BLOCK, (at + 1) * BLOCK)
        gram_ref[rows, lanes] = cov(top, low, high) - gram(top, low, high, 0, depth)

    def tiles(begin, wide):
        first = [(begin, begin + BLOCK)] if (total - begin) % wide else []
        begin += BLOCK * len(first)
        return first + [(at, at + wide) for at in range(begin, total, wide)]

    waiting = []
    for top in range(0, inner, BLOCK):
        end = top + BLOCK
        pivot = cov(top, top, end) + eye_nugget(BLOCK)
        if top > 0:
            pivot = pivot - gram(top, top, end, 0, top)
        tasks = []
        for low, high in tiles(end, 2 * BLOCK):
            tasks += [lambda job=job, low=low, high=high: job(low, high) for job in waiting]
            tasks.append(lambda low=low, high=high: prepare(top, low, high))
        if end == inner:
            for at in range(chosen):
                for low, high in tiles(inner, 3 * BLOCK):
                    tasks.append(lambda at=at, low=low, high=high: partial(at, low, high, top))
        inv_high, inv_low = halves(inverse_factor(pivot, tasks))
        if end < inner:
            solve(top, inv_high, inv_low, end, end + BLOCK)
            waiting = [lambda low, high, top=top, one=inv_high, two=inv_low: solve(top, one, two, low, high)]
        else:
            for low, high in tiles(end, 2 * BLOCK):
                solve(top, inv_high, inv_low, low, high)
    for at in range(chosen):
        top = inner + at * BLOCK
        rows = slice(at * BLOCK, (at + 1) * BLOCK)
        strip = gram_ref[rows, :] - gram(top, inner, total, inner - BLOCK, inner)
        for to in range(chosen):
            out_ref[pl.ds(starts[at], BLOCK), pl.ds(starts[to], BLOCK)] = strip[:, to * BLOCK : (to + 1) * BLOCK]


def schur_scratch(inner, total):
    return [
        pltpu.VMEM((8 * STRIP, total), BF16),
        pltpu.VMEM((8 * STRIP, total), BF16),
        pltpu.VMEM((inner, total), BF16),
        pltpu.VMEM((inner, total), BF16),
        pltpu.VMEM((total, inner), BF16),
        pltpu.VMEM((total, inner), BF16),
        pltpu.VMEM((BLOCK, total), BF16),
        pltpu.VMEM((BLOCK, total), BF16),
        pltpu.VMEM((total - inner, total - inner), F32),
    ]


def schur(points, seps, scales, blocks):
    inner = points.shape[1]
    order = seps.shape[1]
    total = inner + blocks.shape[0] * BLOCK
    vmem = pl.BlockSpec(memory_space=pltpu.VMEM)
    return pl.pallas_call(
        schur_kernel,
        out_shape=jax.ShapeDtypeStruct((order, order), F32),
        in_specs=[pl.BlockSpec(memory_space=pltpu.SMEM), vmem, vmem, vmem],
        out_specs=vmem,
        scratch_shapes=schur_scratch(inner, total),
        compiler_params=pltpu.CompilerParams(vmem_limit_bytes=VMEM_LIMIT),
        name="schur",
    )(blocks, points, seps, scales)


def covariance_rows(left_pts, right_pts, scales, row_start):
    left_scaled = left_pts / scales
    right_scaled = right_pts / scales
    cross = lax.dot_general(
        left_scaled, right_scaled, (((0,), (0,)), ((), ())), precision=HIGHEST, preferred_element_type=F32
    )
    distance = (
        jnp.sum(left_scaled * left_scaled, 0)[:, None]
        + jnp.sum(right_scaled * right_scaled, 0)[None, :]
        - 2.0 * cross
    )
    row_ids = row_start + lax.broadcasted_iota(jnp.int32, cross.shape, 0)
    col_ids = lax.broadcasted_iota(jnp.int32, cross.shape, 1)
    return jnp.exp(-0.5 * distance) + jnp.where(row_ids == col_ids, NUGGET, 0.0)


def level_kernel(lowest, start_ref, gathered_ref, front_ref, cols_ref, reduced_ref, all_ref):
    start = pl.multiple_of(start_ref[0], STRIP)
    rows = front_ref.shape[0]
    inverse = inverse_factor(gathered_ref[lowest : lowest + BLOCK, :])
    all_ref[...] = dot_nt_exact(gathered_ref[...], inverse)
    cols = all_ref[pl.ds(start, rows), :]
    cols_ref[...] = cols
    update = dot_nt_exact(cols, all_ref[...])
    row_ids = start + lax.broadcasted_iota(jnp.int32, update.shape, 0)
    col_ids = lax.broadcasted_iota(jnp.int32, update.shape, 1)
    inside = (row_ids >= lowest) & (row_ids < lowest + BLOCK) | (col_ids >= lowest) & (
        col_ids < lowest + BLOCK
    )
    reduced_ref[...] = jnp.where(inside, 0.0, front_ref[...] - update)


def level(gathered, front_rows, row_start, lowest):
    def run(*refs):
        level_kernel(lowest, *refs)

    vmem = pl.BlockSpec(memory_space=pltpu.VMEM)
    rows = front_rows.shape[0]
    return pl.pallas_call(
        run,
        out_shape=(
            jax.ShapeDtypeStruct((rows, BLOCK), F32),
            jax.ShapeDtypeStruct(front_rows.shape, F32),
        ),
        in_specs=[pl.BlockSpec(memory_space=pltpu.SMEM), vmem, vmem],
        out_specs=(vmem, vmem),
        scratch_shapes=[pltpu.VMEM(gathered.shape, F32)],
        compiler_params=pltpu.CompilerParams(vmem_limit_bytes=VMEM_LIMIT),
        name="level",
    )(row_start.reshape(1), gathered, front_rows)


def schur_split_kernel(blocks_ref, points_ref, seps_ref, scales_ref, first_ref, next_ref, rest_ref, last_ref, sum_ref, *scratch):
    schur_kernel(blocks_ref, points_ref, seps_ref, scales_ref, sum_ref, *scratch)
    half = LEVEL_COUNT * BLOCK
    first_ref[...] = sum_ref[:, :BLOCK]
    next_ref[...] = sum_ref[BLOCK:, BLOCK : 2 * BLOCK]
    rest_ref[...] = sum_ref[2 * BLOCK :, 2 * BLOCK : half]
    last_ref[...] = sum_ref[half:, half:]


def schur_split(points, seps, scales, blocks):
    inner = points.shape[1]
    order = seps.shape[1]
    half = LEVEL_COUNT * BLOCK
    total = inner + blocks.shape[0] * BLOCK
    vmem = pl.BlockSpec(memory_space=pltpu.VMEM)
    return pl.pallas_call(
        schur_split_kernel,
        out_shape=(
            jax.ShapeDtypeStruct((order, BLOCK), F32),
            jax.ShapeDtypeStruct((order - BLOCK, BLOCK), F32),
            jax.ShapeDtypeStruct((order - 2 * BLOCK, half - 2 * BLOCK), F32),
            jax.ShapeDtypeStruct((order - half, order - half), F32),
        ),
        in_specs=[pl.BlockSpec(memory_space=pltpu.SMEM), vmem, vmem, vmem],
        out_specs=(vmem, vmem, vmem, vmem),
        scratch_shapes=[pltpu.VMEM((order, order), F32)] + schur_scratch(inner, total),
        compiler_params=pltpu.CompilerParams(vmem_limit_bytes=VMEM_LIMIT),
        name="schur",
    )(blocks, points, seps, scales)


def clear_rows(value, block_at):
    row_ids = lax.broadcasted_iota(jnp.int32, value.shape, 0)
    low = block_at * BLOCK
    return jnp.where((row_ids >= low) & (row_ids < low + BLOCK), 0.0, value)


def rows_of(ref, block_at):
    return ref[block_at * BLOCK : (block_at + 1) * BLOCK, :]


def dot_nt(left, right):
    left_high, left_low = halves(left)
    right_high, right_low = halves(right)

    def product(one, two):
        return lax.dot_general(one, two, (((1,), (1,)), ((), ())), preferred_element_type=F32)

    return product(left_high, right_high) + product(left_high, right_low) + product(left_low, right_high)


def covariance_block(rows, cols, shift):
    value = jnp.exp(dot_tn(features(rows)[0], features(cols)[1]))
    row_ids = lax.broadcasted_iota(jnp.int32, value.shape, 0)
    col_ids = lax.broadcasted_iota(jnp.int32, value.shape, 1)
    return value + jnp.where(row_ids == col_ids + shift, NUGGET, 0.0)


def column_covariance(points, block_at):
    return covariance_block(points, points[:, block_at * BLOCK : (block_at + 1) * BLOCK], block_at * BLOCK)


def below(value, blocks):
    return jnp.concatenate([jnp.zeros((blocks * BLOCK, value.shape[1]), F32), value], 0)


def level0_kernel(seps_ref, scales_ref, sum_ref, factor_ref):
    column = column_covariance(seps_ref[...] / scales_ref[...], 0) + sum_ref[...]
    factor_ref[...] = dot_nt_exact(column, inverse_factor(column[:BLOCK]))


def first_column(block_at, summed, seps_ref, other_seps_ref, anc_ref, scales_ref, mine_ref, other_ref):
    scales = scales_ref[...]
    value = (
        summed
        + column_covariance(seps_ref[...] / scales, block_at)
        + column_covariance(other_seps_ref[...] / scales, block_at)
        - dot_nt(mine_ref[...], rows_of(mine_ref, block_at))
        - dot_nt(other_ref[...], rows_of(other_ref, block_at))
    )
    return clear_rows(value, 0) + column_covariance(anc_ref[...] / scales, block_at)


def level1_kernel(sum_ref, *refs):
    *refs, factor_ref = refs
    column = first_column(1, below(sum_ref[...], 1), *refs)
    factor_ref[...] = dot_nt_exact(column, inverse_factor(column[BLOCK : 2 * BLOCK]))


def next_kernel(factor_ref, sum_ref, *refs):
    *refs, second_ref, third_ref = refs
    for block_at, out_ref in ((2, second_ref), (3, third_ref)):
        summed = below(sum_ref[:, (block_at - 2) * BLOCK : (block_at - 1) * BLOCK], 2)
        column = first_column(block_at, summed, *refs)
        out_ref[...] = clear_rows(column - dot_nt(factor_ref[...], rows_of(factor_ref, block_at)), 1)


def share_kernel(place_ref, factor_ref, third_ref, last_ref, *refs):
    seps_ref, other_seps_ref, anc_ref, scales_ref, mine_ref, other_ref, own_ref = refs
    at = place_ref[0]
    half = LEVEL_COUNT * BLOCK
    scales = scales_ref[...]
    anc = anc_ref[...] / scales

    @pl.when(at < LEVEL_COUNT)
    def _():
        zero = clear_rows(
            column_covariance(anc, 0) - dot_nt(factor_ref[...], rows_of(factor_ref, 0)), 1
        )
        own_ref[...] = jnp.where(at == 0, zero, jnp.where(at == 3, third_ref[...], 0.0))

    @pl.when(at >= LEVEL_COUNT)
    def _():
        lanes = pl.ds(pl.multiple_of(at * BLOCK, BLOCK), BLOCK)
        anc_here = anc_ref[:, lanes] / scales
        tail = slice(half, None)
        here = factor_ref[lanes, :]
        top = covariance_block(anc[:, :BLOCK], anc_here, -half - BLOCK)
        own_ref[:BLOCK, :] = top - dot_nt(factor_ref[:BLOCK, :], here)
        own_ref[BLOCK : 3 * BLOCK, :] = jnp.zeros((2 * BLOCK, BLOCK), F32)
        own_ref[3 * BLOCK : half, :] = third_ref[lanes, :].T
        shift = at * BLOCK - half
        value = last_ref[...] + covariance_block(anc[:, tail], anc_here, shift)
        value = value - dot_nt(factor_ref[tail, :], here)
        for points_ref in (seps_ref, other_seps_ref):
            value = value + covariance_block(points_ref[:, tail] / scales, points_ref[:, lanes] / scales, shift)
        for one_ref in (mine_ref, other_ref):
            value = value - dot_nt(one_ref[tail, :], one_ref[lanes, :])
        own_ref[tail, :] = value


def level2_kernel(mine_ref, other_ref, anc_ref, scales_ref, factor_ref):
    column = mine_ref[...] + other_ref[...] + column_covariance(anc_ref[...] / scales_ref[...], 2)
    factor_ref[...] = dot_nt_exact(column, inverse_factor(column[2 * BLOCK : 3 * BLOCK]))


def level3_kernel(sum_ref, anc1_ref, anc2_ref, scales_ref, mine_ref, other_ref, factor_ref):
    scales = scales_ref[...]
    value = (
        sum_ref[...]
        + 2.0 * column_covariance(anc1_ref[...] / scales, 3)
        - dot_nt(mine_ref[...], rows_of(mine_ref, 3))
        - dot_nt(other_ref[...], rows_of(other_ref, 3))
    )
    column = clear_rows(value, 2) + column_covariance(anc2_ref[...] / scales, 3)
    factor_ref[...] = dot_nt_exact(column, inverse_factor(column[3 * BLOCK : 4 * BLOCK]))


def top_kernel(start_ref, sum_ref, ancs_ref, scales_ref, mine_ref, other_ref, last_ref, out_ref):
    start = pl.multiple_of(start_ref[0], BLOCK)
    shape = out_ref.shape
    scales = scales_ref[...]
    row_ids = start + lax.broadcasted_iota(jnp.int32, shape, 0)
    col_ids = lax.broadcasted_iota(jnp.int32, shape, 1)

    def inside(block_at):
        low, high = block_at * BLOCK, (block_at + 1) * BLOCK
        return (row_ids >= low) & (row_ids < high) | (col_ids >= low) & (col_ids < high)

    def ancestor(level_at):
        rows = ancs_ref[level_at, :, pl.ds(start, shape[0])] / scales
        return covariance_block(rows, ancs_ref[level_at] / scales, -start)

    def product(ref):
        return dot_nt(ref[pl.ds(start, shape[0]), :], ref[...])

    summed = jnp.concatenate(
        [sum_ref[core, side, pair] for pair in range(2) for core in range(2) for side in range(2)], 1
    )
    value = summed + 2.0 * ancestor(1) - product(mine_ref) - product(other_ref)
    value = jnp.where(inside(2), 0.0, value) + ancestor(2) - product(last_ref)
    out_ref[...] = 2.0 * jnp.where(inside(3), 0.0, value) + ancestor(3)


def local_call(kernel, name, shapes, *operands, scalar=None, micros=2):
    vmem = pl.BlockSpec(memory_space=pltpu.VMEM)
    in_specs = [vmem] * len(operands)
    if scalar is not None:
        in_specs = [pl.BlockSpec(memory_space=pltpu.SMEM)] + in_specs
        operands = (scalar.reshape(1),) + operands
    outs = tuple(jax.ShapeDtypeStruct(shape, F32) for shape in shapes)
    return pl.pallas_call(
        kernel,
        out_shape=outs,
        in_specs=in_specs,
        out_specs=(vmem,) * len(outs),
        compiler_params=pltpu.CompilerParams(vmem_limit_bytes=VMEM_LIMIT),
        cost_estimate=pl.CostEstimate(flops=micros * 10**9, bytes_accessed=2**20, transcendentals=0),
        name=name,
    )(*operands)


def cut(value, start, size, axis=0):
    return lax.dynamic_slice_in_dim(value, start, size, axis)


def grouped_body(interior_points, sep_points, anc_points, scales, block_map):
    order = sep_points.shape[2]
    design = sep_points.shape[1]
    inner = interior_points.shape[2]
    chosen = block_map.shape[1]
    leaves, panels = lax.axis_size("leaf"), lax.axis_size("panel")
    place, panel = lax.axis_index("leaf"), lax.axis_index("panel")
    core, side, pair = place % 2, place // 2 % 2, place // 4
    half, rows = order // 2, order // panels
    scales = scales[:, None]
    tall = [(order, BLOCK)]

    def flip(value, bit):
        return lax.ppermute(value, "leaf", [(at, at ^ bit) for at in range(leaves)])

    def across(value, bit):
        return lax.ppermute(value, "panel", [(at, at ^ bit) for at in range(panels)])

    def target(leaf, piece):
        return (4 * (leaf % 2) + piece) * panels + leaf // 2

    def route(change):
        return [
            (leaf * panels + piece, target(leaf ^ change, piece))
            for leaf in range(leaves)
            for piece in range(panels)
        ]

    def share(part):
        other = flip(part, 1)
        return jnp.where(core == 0, jnp.concatenate([part, other]), jnp.concatenate([other, part]))

    def my_half(value):
        size = value.shape[0] // 2
        return cut(value, core * size, size)

    def core_sum(value):
        size = value.shape[0] // 2
        return my_half(value) + flip(cut(value, (1 - core) * size, size), 1)

    def group_sum(part, bits):
        for bit in bits:
            part = part + flip(part, bit)
        return share(part)

    names = jnp.pad(block_map.astype(F32), ((0, design - 1), (0, BLOCK - chosen)))
    packed = jnp.concatenate([interior_points[0], sep_points[0], names], 1)
    packed = lax.ppermute(packed, ("leaf", "panel"), route(0))
    points, seps = packed[:, :inner], packed[:, inner : inner + order]
    blocks = packed[0, inner + order : inner + order + chosen].astype(jnp.int32)
    first, second, rest, last = schur_split(points, seps, scales, blocks)
    other_seps = lax.ppermute(sep_points[0], ("leaf", "panel"), route(1))

    first, second, rest, last = lax.optimization_barrier((core_sum(first), second, rest, last))
    second, rest = core_sum(second), core_sum(rest)
    first = first + flip(first, 2)
    first, second, rest = lax.optimization_barrier((first, second, rest))
    (factor0,) = local_call(level0_kernel, "level0", tall, seps, scales, share(first), micros=6)
    second = group_sum(second, (2, 4))
    rest = group_sum(rest, (4, 2))
    other0 = share(flip(my_half(factor0), 4))
    shared = (seps, other_seps, anc_points[0], scales, factor0, other0)
    (factor1,) = local_call(level1_kernel, "level1", tall, second, *shared, micros=7)
    reduced2, reduced3 = local_call(next_kernel, "next1", tall + tall, factor1, rest, *shared)
    arrived2 = share(across(my_half(reduced2), 1))
    width = (order - half) // 2
    piece = cut(last, core * width, width, 1) + flip(cut(last, (1 - core) * width, width, 1), 1)
    piece, _ = lax.optimization_barrier((piece, factor0))
    width //= 2
    piece = cut(piece, side * width, width, 1) + flip(cut(piece, (1 - side) * width, width, 1), 2)
    piece = piece + flip(piece, 4)
    column_at = 4 * pair + 2 * core + side
    (own,) = local_call(
        share_kernel, "share1", tall, factor1, reduced3, piece, *shared, scalar=column_at, micros=3
    )

    def my_quarter(value):
        value = my_half(value)
        size = value.shape[0] // 2
        return cut(value, side * size, size)

    def share_quarter(part):
        other = flip(part, 2)
        return share(jnp.where(side == 0, jnp.concatenate([part, other]), jnp.concatenate([other, part])))

    summed3 = my_quarter(reduced3)
    summed3 = summed3 + across(summed3, 1)
    (factor2,) = local_call(
        level2_kernel, "level2", tall, reduced2, arrived2, anc_points[1], scales, micros=6
    )
    summed3 = share_quarter(summed3 + across(summed3, 2))
    partner2 = share_quarter(across(my_quarter(factor2), 2))
    (factor3,) = local_call(
        level3_kernel,
        "level3",
        tall,
        summed3,
        anc_points[1],
        anc_points[2],
        scales,
        factor2,
        partner2,
        micros=7,
    )
    own = lax.psum_scatter(own, "panel", scatter_dimension=0, tiled=True)
    for at, bit in ((pair, 4), (side, 2), (core, 1)):
        other = flip(own, bit)
        own = jnp.where(at == 0, jnp.stack([own, other]), jnp.stack([other, own]))
    start = panel * rows
    (top,) = local_call(
        top_kernel,
        "top",
        [(rows, order)],
        own,
        anc_points,
        scales,
        factor2,
        partner2,
        factor3,
        scalar=start,
    )
    piece_at = (place % 4) * rows
    early = lax.ppermute(
        jnp.stack([cut(factor0, piece_at, rows), cut(factor1, piece_at, rows)]),
        ("leaf", "panel"),
        [(at, to) for to, at in route(0)],
    )
    late = jnp.stack([cut(jnp.where(panel // 2 == pair, factor2, partner2), start, rows), cut(factor3, start, rows)])
    return (jnp.concatenate([early, late])[None], top[None])


def body(interior_points, sep_points, anc_points, scales, block_map):
    order = sep_points.shape[2]
    panels = lax.axis_size("panel")
    row_count = order // panels
    row_start = lax.axis_index("panel") * row_count
    seps = sep_points[0]
    scales = scales[:, None]
    placed = schur(interior_points[0], seps, scales, block_map[0])
    summed = lax.psum_scatter(placed, "panel", scatter_dimension=0, tiled=True)
    local_seps = lax.dynamic_slice_in_dim(seps, row_start, row_count, 1)
    front_rows = covariance_rows(local_seps, seps, scales, row_start) + summed
    levels = anc_points.shape[0]
    ancestors = []
    for level_at in range(levels):
        local_anc = lax.dynamic_slice_in_dim(anc_points[level_at], row_start, row_count, 1)
        ancestors.append(covariance_rows(local_anc, anc_points[level_at], scales, row_start))
    bit_count = lax.axis_size("leaf").bit_length() - 1
    factors = []
    for level_at in range(levels):
        lowest = level_at * BLOCK
        gathered = lax.all_gather(
            front_rows[:, lowest : lowest + BLOCK], "panel", axis=0, tiled=True
        )
        cols_rows, reduced = level(gathered, front_rows, row_start, lowest)
        partner = partner_2(reduced, "leaf", level_at % bit_count)
        front_rows = reduced + partner + ancestors[level_at]
        factors.append(cols_rows)
    return (jnp.stack(factors, 0)[None], front_rows[None])


def solution(mesh):
    in_specs = (P("leaf", None, "panel"), P("leaf", None, None), P(), P(), P("leaf", "panel"))
    out_specs = (P("leaf", None, "panel", None), P("leaf", "panel", None))
    sizes = mesh.shape["leaf"], mesh.shape["panel"]
    chosen = grouped_body if sizes == (8, 4) else body
    return jax.shard_map(chosen, mesh=mesh, in_specs=in_specs, out_specs=out_specs, check_vma=False)
```
